256 devices in a mesh: section: 32 (over z, x_lo, core), tp: 8 (over y, x_hi).
Axes of the slice: x: 4 (x_hi: 2, x_lo: 2; x = x_hi * 2 + x_lo), y: 4, z: 8, core: 2. Of those that a mesh axis runs over, the one named last changes fastest.
Arguments:
- weights: bfloat16 [32, 1024, 8192], P('section', 'tp'), may hold values from -0.5 to 0.5
- mirror_weights: bfloat16 [32, 1024, 8192], P('section', 'tp'), may hold values from -0.5 to 0.5
- acts_down: bfloat16 [32, 256, 8192], P('section', None, 'tp'), may hold values from -8 to 8
- cot_down: bfloat16 [32, 256, 8192], P('section', None, 'tp'), may hold values from -6 to 6
- key_cotangent_lower: bfloat16 [32, 256, 1024], P('section', None, 'tp'), may hold values from -6 to 6
- acts_up: bfloat16 [32, 256, 8192], P('section', None, 'tp'), may hold values from -8 to 8
- cot_up: bfloat16 [32, 256, 8192], P('section', None, 'tp'), may hold values from -6 to 6
- key_cot_up: bfloat16 [32, 256, 1024], P('section', None, 'tp'), may hold values from -6 to 6
Outputs:
- weight_grad: bfloat16 [32, 1024, 8192], P('section', 'tp')
- grad_down: bfloat16 [32, 256, 8192], P('section', None, 'tp')
- grad_up: bfloat16 [32, 256, 8192], P('section', None, 'tp')
The draws below stay inside these ranges and needn't reach their ends.
All inputs are finite; a program needn't handle non-finite values.
Results may differ from the reference program's by a relative error of at most 0.014.
Values may be sent and summed in bfloat16 or wider, within the bound.
A program may use at most 192 MiB of HBM per device.

```python
import math
import jax
import jax.numpy as jnp
from jax import lax

D = 8192
KV = 1024
TOK = 256
SECTIONS = 32
N_TP = 8


def feature_profile(key, rise):
    profile_key = jax.random.fold_in(key, 100)
    position = jnp.arange(D, dtype=jnp.float32) / D
    magnitude = jnp.exp(rise * position) * jax.random.uniform(profile_key, (D,), jnp.float32, 0.5, 1.5)
    signs = (2 * jax.random.randint(jax.random.fold_in(profile_key, 1), (D,), 0, 2) - 1).astype(jnp.float32)
    mean_square = (math.exp(2.0 * rise) - 1.0) / (2.0 * rise) * (13.0 / 12.0)
    return signs * magnitude / math.sqrt(mean_square)


def projection_draw(key, own_constant, rise):
    profile = feature_profile(key, rise)
    key = jax.random.fold_in(key, own_constant)
    noise_key, coef_key = jax.random.split(key)
    noise = jax.random.normal(noise_key, (SECTIONS, KV, D), jnp.float32) / math.sqrt(KV)
    coef = jax.random.normal(coef_key, (SECTIONS, KV, 1), jnp.float32) * (0.7 / math.sqrt(KV))
    return jnp.clip(noise + coef * profile, -0.5, 0.5)


def input_draw(key, own_constant, rise):
    profile = feature_profile(key, rise)
    key = jax.random.fold_in(key, own_constant)
    noise_key, coef_key = jax.random.split(key)
    noise = jax.random.normal(noise_key, (SECTIONS, TOK, D), jnp.float32)
    coef = jax.random.normal(coef_key, (SECTIONS, TOK, 1), jnp.float32)
    return jnp.clip(noise + coef * profile, -8.0, 8.0)


def draw_weights(key, part):
    rise = 0.9
    return projection_draw(key, 3, rise).astype(jnp.bfloat16)


def draw_mirror_weights(key, part):
    rise = 0.9
    return projection_draw(key, 4, rise).astype(jnp.bfloat16)


def draw_acts_down(key, part):
    rise = 0.9
    return input_draw(key, 5, rise).astype(jnp.bfloat16)


def draw_acts_up(key, part):
    rise = 0.9
    return input_draw(key, 6, rise).astype(jnp.bfloat16)


def steps_of(stream_key, dims, cuts, smallest, high):
    loudness, own = 1.0, jax.random.fold_in(stream_key, 6)
    for dim, blocks in cuts:
        heights = jnp.exp(jax.random.uniform(jax.random.fold_in(own, dim), (blocks,), jnp.float32, smallest / len(cuts), high / len(cuts)))
        loudness = loudness * jnp.repeat(heights, dims[dim] // blocks).reshape([-1 if axis == dim else 1 for axis in range(len(dims))])
    return loudness


def centred(rng, extent, width, bound, pieces=(), kind=jnp.bfloat16):
    array = width * jax.random.normal(rng, extent, jnp.float32)
    if pieces:
        array = array * steps_of(rng, extent, pieces, -0.22, 0.18)
    return jnp.clip(array, -bound, bound).astype(kind)


def setup_inputs(seed: int = 0) -> dict:
    streams_of = jax.random.split(jax.random.key(seed), 9)
    weights = draw_weights(jax.random.fold_in(streams_of[8], 71), 0)
    mirror_weights = draw_mirror_weights(jax.random.fold_in(streams_of[8], 71), 0)
    acts_down = draw_acts_down(jax.random.fold_in(streams_of[8], 71), 0)
    cot_down = centred(streams_of[3], (SECTIONS, TOK, D), 1.0, 6.0, ((0, 32), (2, 8)))
    key_cotangent_lower = centred(streams_of[4], (SECTIONS, TOK, KV), 1.0, 6.0, ((0, 32), (2, 8)))
    acts_up = draw_acts_up(jax.random.fold_in(streams_of[8], 71), 0)
    cot_up = centred(streams_of[6], (SECTIONS, TOK, D), 1.0, 6.0, ((0, 32), (2, 8)))
    key_cot_up = centred(streams_of[7], (SECTIONS, TOK, KV), 1.0, 6.0, ((0, 32), (2, 8)))
    return {"weights": weights, "mirror_weights": mirror_weights, "acts_down": acts_down, "cot_down": cot_down, "key_cotangent_lower": key_cotangent_lower, "acts_up": acts_up, "cot_up": cot_up, "key_cot_up": key_cot_up}


epsilon = 1e-05

def section_backward(weight, rows_x, rows_c, rows_g):
    inputs = rows_x.astype(jnp.float32)
    inv_rms = lax.rsqrt(lax.optimization_barrier(jnp.mean(inputs * inputs, axis=1, keepdims=True)) + epsilon)
    normed = inputs * inv_rms
    normed_half = normed.astype(jnp.bfloat16)
    key_grad = jnp.dot(rows_g.T, normed_half, preferred_element_type=jnp.float32)
    row_count = rows_x.shape[0]
    group_cotangent = rows_g.reshape(row_count, N_TP, KV // N_TP).transpose(1, 0, 2).astype(jnp.float32)
    group_weight_matrix = weight.reshape(N_TP, KV // N_TP, D).astype(jnp.float32)
    partial_terms = jnp.einsum('atb,abk->atk', group_cotangent, group_weight_matrix, precision=lax.Precision.HIGHEST)
    rounded = lax.optimization_barrier(partial_terms.astype(jnp.bfloat16))
    hidden_grad = lax.optimization_barrier(jnp.sum(rounded.astype(jnp.float32), axis=0))
    row_dots = lax.optimization_barrier(jnp.mean(hidden_grad * normed, axis=1, keepdims=True))
    result = rows_c.astype(jnp.float32) + inv_rms * (hidden_grad - normed * row_dots)
    return (key_grad, result.astype(jnp.bfloat16))

def reference(weights, mirror_weights, acts_down, cot_down, key_cotangent_lower, acts_up, cot_up, key_cot_up):

    def per_section(items):
        weight, near_x, near_c, near_g, far_weight, far_x, far_c, far_g = items
        nearby_key, near_out = section_backward(weight, near_x, near_c, near_g)
        far_key, distant_output = section_backward(far_weight, far_x, far_c, far_g)
        far_half = lax.optimization_barrier(far_key.astype(jnp.bfloat16))
        total = nearby_key + far_half.astype(jnp.float32)
        return (total.astype(jnp.bfloat16), near_out, distant_output)
    grads, near_out, distant_output = lax.map(per_section, (weights, acts_down, cot_down, key_cotangent_lower, mirror_weights[::-1], acts_up[::-1], cot_up[::-1], key_cot_up[::-1]))
    zero_block = jnp.zeros((1, TOK, D), jnp.bfloat16)
    grad_down = jnp.concatenate([near_out[1:], zero_block], axis=0)
    flipped = distant_output[::-1]
    grad_up = jnp.concatenate([zero_block, flipped[:-1]], axis=0)
    return (grads, grad_down, grad_up)
```

```python
import functools

import jax
import jax.numpy as jnp
from jax import lax
from jax.experimental import pallas as pl
from jax.experimental.pallas import tpu as pltpu
from jax.sharding import PartitionSpec as P

epsilon = 1e-05
MESH = pl.DeviceIdType.MESH
F32 = jnp.float32
BF16 = jnp.bfloat16
N_SEMS = 56


def kernel(
    n_sections,
    w_ref,
    mw_ref,
    xd_ref,
    cd_ref,
    gd_ref,
    xu_ref,
    cu_ref,
    gu_ref,
    wg_ref,
    down_ref,
    up_ref,
    w_all,
    g_all,
    g_scaled,
    x_all,
    x_far,
    c_own,
    part_send,
    part_recv,
    hidden,
    key_send,
    result,
    lanes,
    squares,
    dots,
    ssem,
    rsem,
    lsem,
):
    tok, width = x_far.shape
    keys = gd_ref.shape[2]
    features = width * 8
    tile = min(256, width)
    s = lax.axis_index("section")
    t = lax.axis_index("tp")
    y = t // 2
    h = t % 2
    pair = (s, t + 1 - 2 * h)
    y_peers = [(s, lax.rem(y + k, 4) * 2 + h) for k in range(1, 4)]
    t_peers = [(s, lax.rem(t + k, 8)) for k in range(1, 8)]
    mirror = n_sections - 1 - s
    mirrors = [(mirror, t), (mirror, t + 1 - 2 * h)]
    behind = (lax.rem(s + n_sections - 1, n_sections), t)
    ahead = (lax.rem(s + 1, n_sections), t)

    everyone = t_peers + mirrors + [behind, ahead]
    barrier = pltpu.get_barrier_semaphore()
    for device in everyone:
        pl.semaphore_signal(barrier, inc=1, device_id=device, device_id_type=MESH)

    used = [0]
    used_local = [0]

    def remote(src, dst, device):
        i = used[0]
        used[0] += 1
        return pltpu.make_async_remote_copy(
            src_ref=src,
            dst_ref=dst,
            send_sem=ssem.at[i],
            recv_sem=rsem.at[i],
            device_id=device,
            device_id_type=MESH,
        )

    def local(src, dst):
        i = used_local[0]
        used_local[0] += 1
        copy = pltpu.make_async_copy(src, dst, lsem.at[i])
        copy.start()
        return copy

    def start(copies):
        for copy in copies:
            copy.start()
        return copies

    def wait_recv(copies):
        for copy in copies:
            copy.wait_recv()

    def wait(copies):
        for copy in copies:
            copy.wait()

    own_x = x_all.at[h, pl.ds(0, tok)]
    own_rows = [own_x, x_far]
    copies_x = [local(xd_ref.at[0], own_x), local(xu_ref.at[0], x_far)]
    my_keys = pl.ds(pl.multiple_of(y * keys, keys), keys)
    copies_g = [
        local(gd_ref.at[0], g_all.at[0, :, my_keys]),
        local(gu_ref.at[0], g_all.at[1, :, my_keys]),
    ]
    w_refs = [w_ref, mw_ref]
    halves = [1 - h, h]

    def w_columns(row, half):
        return pl.ds(pl.multiple_of((row * 2 + half) * width, width), width)

    copies_w = [
        [local(w_refs[m].at[0, :, w_columns(y, half)], w_all.at[m, i, my_keys]) for m in range(2)]
        for i, half in enumerate(halves)
    ]
    copies_c = [local(cd_ref.at[0], c_own.at[0]), local(cu_ref.at[0], c_own.at[1])]

    pl.semaphore_wait(barrier, len(everyone))

    g_sends = start(
        [
            remote(ref.at[0], g_all.at[m, :, my_keys], device)
            for m, ref in enumerate((gd_ref, gu_ref))
            for device in y_peers
        ]
    )

    def w_sends(i, m):
        return start(
            [
                remote(
                    w_refs[m].at[0, :, w_columns(lax.rem(y + k + 1, 4), halves[i])],
                    w_all.at[m, i, my_keys],
                    y_peers[k],
                )
                for k in range(3)
            ]
        )

    w_chunks = [w_sends(0, 0), w_sends(0, 1)]
    x_sends = start(
        [
            remote(xd_ref.at[0], x_all.at[h, pl.ds(0, tok)], pair),
            remote(xu_ref.at[0], x_all.at[h, pl.ds(tok, tok)], mirrors[0]),
            remote(xu_ref.at[0], x_all.at[h, pl.ds(tok, tok)], mirrors[1]),
        ]
    )

    def to_row(m):
        return jnp.sum(jnp.transpose(lanes[m]), axis=0, keepdims=True)

    def fold(values):
        total = values[:, :128]
        for i in range(1, values.shape[1] // 128):
            total = total + values[:, i * 128 : (i + 1) * 128]
        return total

    def share(buffer, rows):
        buffer[t] = jnp.broadcast_to(rows, buffer.shape[1:])
        return start([remote(buffer.at[t], buffer.at[t], device) for device in t_peers])

    def total_of(buffer):
        total = buffer[0]
        for i in range(1, 8):
            total = total + buffer[i]
        return total[:1]

    row_block = min(64, tok)
    for m in range(2):
        copies_x[m].wait()

        @pl.loop(0, tok // row_block)
        def _(i):
            rows = pl.ds(pl.multiple_of(i * row_block, row_block), row_block)
            if m == 0:
                values = x_all[h, rows].astype(F32)
            else:
                values = x_far[rows].astype(F32)
            lanes[m, rows] = fold(values * values)

    square_sends = share(squares, jnp.concatenate([to_row(0), to_row(1)], axis=1))

    wait(copies_g)
    wait_recv(g_sends)

    def partial(m, i, use):
        copies_w[i][m].wait()
        wait_recv(w_chunks[i * 2 + m])

        @pl.loop(0, width // tile)
        def _(j):
            columns = pl.ds(pl.multiple_of(j * tile, tile), tile)
            use(columns, jnp.dot(g_all[m], w_all[m, i, :, columns], preferred_element_type=F32))

    part_sends = []
    for m in range(2):

        def keep(columns, value):
            part_send[m, :, columns] = value.astype(BF16)

        partial(m, 0, keep)
        part_sends += start([remote(part_send.at[m], part_recv.at[m], pair)])
        w_chunks.append(w_sends(1, m))

    wait_recv(square_sends)
    inv_rms = lax.rsqrt(total_of(squares) / features + epsilon)
    for m in range(2):
        scale = inv_rms[:, m * tok : (m + 1) * tok]
        for k in range(4):
            block = jnp.transpose(g_all[m, :, k * keys : (k + 1) * keys].astype(F32))
            g_scaled[m, k * keys : (k + 1) * keys] = (block * scale).astype(BF16)
    g_far = start([remote(g_scaled.at[1], g_scaled.at[2], mirrors[0])])

    key_sends = []
    key_own = []

    def key_half(half):
        @pl.loop(0, width // tile)
        def _(j):
            columns = pl.ds(pl.multiple_of(j * tile, tile), tile)
            value = jnp.dot(g_scaled[0], x_all[half, :tok, columns], preferred_element_type=F32)
            value += jnp.dot(g_scaled[2], x_all[half, tok:, columns], preferred_element_type=F32)
            key_send[half, :, columns] = value.astype(BF16)

        place = wg_ref.at[0, :, w_columns(y, half)]
        for k in range(3):
            rows = pl.ds(pl.multiple_of(lax.rem(y + k + 1, 4) * keys, keys), keys)
            key_sends.extend(start([remote(key_send.at[half, rows], place, y_peers[k])]))
        key_own.append(local(key_send.at[half, my_keys], place))

    copies_x_in = x_sends
    wait_recv(copies_x_in)
    wait_recv(g_far)
    key_half(0)

    for m in range(2):

        def finish(columns, value):
            if m == 0:
                x_rows = x_all[h, :tok, columns]
            else:
                x_rows = x_far[:, columns]
            value = value + part_recv[m, :, columns].astype(F32)
            hidden[m, :, columns] = value
            lanes[m] += fold(value * x_rows.astype(F32))

        lanes[m] = jnp.zeros_like(lanes[m])
        part_sends[m].wait_recv()
        partial(m, 1, finish)
    dot_sends = share(dots, jnp.concatenate([to_row(0), to_row(1)], axis=1))
    key_half(1)

    wait(copies_c)
    wait_recv(dot_sends)
    slope = total_of(dots) * (inv_rms * inv_rms * inv_rms) / features

    def to_column(row):
        return jnp.transpose(jnp.broadcast_to(row, (128, row.shape[1])))

    shift_sends = []
    outs = [down_ref, up_ref]
    kept = [s > 0, s < n_sections - 1]
    for m in range(2):
        lanes[0] = to_column(inv_rms[:, m * tok : (m + 1) * tok])
        lanes[1] = to_column(slope[:, m * tok : (m + 1) * tok])

        @pl.loop(0, tok // row_block)
        def _(i):
            rows = pl.ds(pl.multiple_of(i * row_block, row_block), row_block)
            if m == 0:
                x_rows = x_all[h, rows].astype(F32)
            else:
                x_rows = x_far[rows].astype(F32)
            value = c_own[m, rows].astype(F32) + (
                hidden[m, rows] * lanes[0, rows, :1] - x_rows * lanes[1, rows, :1]
            )
            result[m, rows] = jnp.where(kept[m], value, 0.0).astype(BF16)

        shift_sends += start([remote(result.at[m], outs[m].at[0], (behind, ahead)[m])])

    wait_recv(shift_sends)
    wait_recv(key_sends)
    wait(key_own)
    groups = [g_sends, x_sends, square_sends, part_sends, g_far, key_sends, dot_sends, shift_sends] + w_chunks
    for group in groups:
        for copy in group:
            copy.wait_send()


def per_device(*args, n_sections):
    w, _, xd, _, gd = args[:5]
    tok, width = xd.shape[1:]
    keys = gd.shape[2]
    any_spec = pl.BlockSpec(memory_space=pl.ANY)
    vmem = pltpu.VMEM
    outs = pl.pallas_call(
        functools.partial(kernel, n_sections),
        out_shape=(
            jax.ShapeDtypeStruct(w.shape, BF16),
            jax.ShapeDtypeStruct(xd.shape, BF16),
            jax.ShapeDtypeStruct(xd.shape, BF16),
        ),
        in_specs=[any_spec] * 8,
        out_specs=(any_spec,) * 3,
        scratch_shapes=[
            vmem((2, 2, 4 * keys, width), BF16),
            vmem((2, tok, 4 * keys), BF16),
            vmem((3, 4 * keys, tok), BF16),
            vmem((2, 2 * tok, width), BF16),
            vmem((tok, width), BF16),
            vmem((2, tok, width), BF16),
            vmem((2, tok, width), BF16),
            vmem((2, tok, width), BF16),
            vmem((2, tok, width), F32),
            vmem((2, 4 * keys, width), BF16),
            vmem((2, tok, width), BF16),
            vmem((2, tok, 128), F32),
            vmem((8, 8, 2 * tok), F32),
            vmem((8, 8, 2 * tok), F32),
            pltpu.SemaphoreType.DMA((N_SEMS,)),
            pltpu.SemaphoreType.DMA((N_SEMS,)),
            pltpu.SemaphoreType.DMA((16,)),
        ],
        compiler_params=pltpu.CompilerParams(
            collective_id=0, has_side_effects=True, vmem_limit_bytes=40 * 2**20
        ),
        name="relay_backward",
    )(*args)
    return outs


def solution(mesh):
    keys_split = P("section", "tp", None)
    features_split = P("section", None, "tp")
    return jax.shard_map(
        functools.partial(per_device, n_sections=mesh.shape["section"]),
        mesh=mesh,
        in_specs=(keys_split,) * 2 + (features_split,) * 6,
        out_specs=(keys_split, features_split, features_split),
        check_vma=False,
    )
```

```python
import functools

import jax
import jax.numpy as jnp
from jax import lax
from jax.experimental import pallas as pl
from jax.experimental.pallas import tpu as pltpu
from jax.sharding import PartitionSpec as P

epsilon = 1e-05
MESH = pl.DeviceIdType.MESH
PIECES = 4
DEPTH = 2
F32 = jnp.float32
BF16 = jnp.bfloat16
N_SEMS = 96


def kernel(
    n_sections,
    w_ref,
    mw_ref,
    xd_ref,
    cd_ref,
    gd_ref,
    xu_ref,
    cu_ref,
    gu_ref,
    wg_ref,
    down_ref,
    up_ref,
    w_all,
    g_all,
    g_scaled,
    x_all,
    x_far,
    c_own,
    part_send,
    part_recv,
    hidden,
    key_send,
    result,
    lanes,
    squares,
    dots,
    ssem,
    rsem,
    lsem,
):
    tok, width = x_far.shape
    keys = gd_ref.shape[2]
    features = width * 8
    tile = min(256, width)
    groups = 2 * tok // 128
    s = lax.axis_index("section")
    t = lax.axis_index("tp")
    y = t // 2
    h = t % 2
    pair = (s, t + 1 - 2 * h)
    y_peers = [(s, lax.rem(y + k, 4) * 2 + h) for k in range(1, 4)]
    t_peers = [(s, lax.rem(t + k, 8)) for k in range(1, 8)]
    mirror = n_sections - 1 - s
    mirrors = [(mirror, t), (mirror, t + 1 - 2 * h)]
    behind = (lax.rem(s + n_sections - 1, n_sections), t)
    ahead = (lax.rem(s + 1, n_sections), t)

    everyone = t_peers + mirrors + [behind, ahead]
    barrier = pltpu.get_barrier_semaphore()
    for device in everyone:
        pl.semaphore_signal(barrier, inc=1, device_id=device, device_id_type=MESH)

    used = [0]
    used_local = [0]

    def remote(src, dst, device):
        i = used[0]
        used[0] += 1
        return pltpu.make_async_remote_copy(
            src_ref=src,
            dst_ref=dst,
            send_sem=ssem.at[i],
            recv_sem=rsem.at[i],
            device_id=device,
            device_id_type=MESH,
        )

    def local(src, dst):
        i = used_local[0]
        used_local[0] += 1
        copy = pltpu.make_async_copy(src, dst, lsem.at[i])
        copy.start()
        return copy

    def start(copies):
        for copy in copies:
            copy.start()
        return copies

    def wait_recv(copies):
        for copy in copies:
            copy.wait_recv()

    def wait(copies):
        for copy in copies:
            copy.wait()

    own_x = x_all.at[h, pl.ds(0, tok)]
    own_rows = [own_x, x_far]
    copies_x = [local(xd_ref.at[0], own_x), local(xu_ref.at[0], x_far)]
    my_keys = pl.ds(pl.multiple_of(y * keys, keys), keys)
    copies_g = [
        local(gd_ref.at[0], g_all.at[0, :, my_keys]),
        local(gu_ref.at[0], g_all.at[1, :, my_keys]),
    ]
    w_refs = [w_ref, mw_ref]
    halves = [1 - h, h]

    def w_columns(row, half):
        return pl.ds(pl.multiple_of((row * 2 + half) * width, width), width)

    copies_w = [
        [local(w_refs[m].at[0, :, w_columns(y, half)], w_all.at[m, i, my_keys]) for m in range(2)]
        for i, half in enumerate(halves)
    ]
    copies_c = [local(cd_ref.at[0], c_own.at[0]), local(cu_ref.at[0], c_own.at[1])]

    pl.semaphore_wait(barrier, len(everyone))

    x_sends = start(
        [
            remote(xd_ref.at[0], x_all.at[h, pl.ds(0, tok)], pair),
            remote(xu_ref.at[0], x_all.at[h, pl.ds(tok, tok)], mirrors[0]),
            remote(xu_ref.at[0], x_all.at[h, pl.ds(tok, tok)], mirrors[1]),
        ]
    )

    g_sends = start(
        [
            remote(ref.at[0], g_all.at[m, :, my_keys], device)
            for m, ref in enumerate((gd_ref, gu_ref))
            for device in y_peers
        ]
    )

    def w_sends(i, m):
        return start(
            [
                remote(
                    w_refs[m].at[0, :, w_columns(lax.rem(y + k + 1, 4), halves[i])],
                    w_all.at[m, i, my_keys],
                    y_peers[k],
                )
                for k in range(3)
            ]
        )

    w_chunks = [w_sends(0, 0), w_sends(0, 1)]
    def to_row(m):
        return jnp.sum(jnp.transpose(lanes[m]), axis=0, keepdims=True)

    def fold(values):
        total = values[:, :128]
        for i in range(1, values.shape[1] // 128):
            total = total + values[:, i * 128 : (i + 1) * 128]
        return total

    def share(buffer, row):
        buffer[t, :groups] = jnp.concatenate([row[:, i * 128 : (i + 1) * 128] for i in range(groups)], axis=0)
        return start([remote(buffer.at[t], buffer.at[t], device) for device in t_peers])

    def total_of(buffer):
        total = buffer[0]
        for i in range(1, 8):
            total = total + buffer[i]
        return jnp.concatenate([total[i : i + 1] for i in range(groups)], axis=1)

    row_block = min(64, tok)
    for m in range(2):
        copies_x[m].wait()

        @pl.loop(0, tok // row_block)
        def _(i):
            rows = pl.ds(pl.multiple_of(i * row_block, row_block), row_block)
            if m == 0:
                values = x_all[h, rows].astype(F32)
            else:
                values = x_far[rows].astype(F32)
            lanes[m, rows] = fold(values * values)

    square_sends = share(squares, jnp.concatenate([to_row(0), to_row(1)], axis=1))

    wait(copies_g)
    wait_recv(g_sends)

    def partial(m, i, use):
        copies_w[i][m].wait()
        if (m, i) != (1, 1):
            wait_recv(w_chunks[i * 2 + m])

        @pl.loop(0, width // tile)
        def _(j):
            columns = pl.ds(pl.multiple_of(j * tile, tile), tile)
            use(columns, jnp.dot(g_all[m], w_all[m, i, :, columns], preferred_element_type=F32))

    part_sends = []
    for m in range(2):
      def keep(columns, value):
          part_send[m, :, columns] = value.astype(BF16)
      partial(m, 0, keep)
      part_sends += start([remote(part_send.at[m], part_recv.at[m], pair)])
      w_chunks.append(w_sends(1, m))

    wait_recv(square_sends)
    inv_rms = lax.rsqrt(total_of(squares) / features + epsilon)
    for m in range(2):
        scale = inv_rms[:, m * tok : (m + 1) * tok]
        for k in range(4):
            block = jnp.transpose(g_all[m, :, k * keys : (k + 1) * keys].astype(F32))
            g_scaled[m, k * keys : (k + 1) * keys] = (block * scale).astype(BF16)
    g_far = start([remote(g_scaled.at[1], g_scaled.at[2], mirrors[0])])

    def own_half(m):
        def finish(columns, value):
            if m == 0:
                x_rows = x_all[h, :tok, columns]
            else:
                x_rows = x_far[:, columns]
            value = value + part_recv[m, :, columns].astype(F32)
            hidden[m, :, columns] = value
            lanes[m] += fold(value * x_rows.astype(F32))

        lanes[m] = jnp.zeros_like(lanes[m])
        part_sends[m].wait_recv()
        partial(m, 1, finish)

    def key_half(half):
        @pl.loop(0, width // tile)
        def _(j):
            columns = pl.ds(pl.multiple_of(j * tile, tile), tile)
            value = jnp.dot(g_scaled[0], x_all[half, :tok, columns], preferred_element_type=F32)
            value += jnp.dot(g_scaled[2], x_all[half, tok:, columns], preferred_element_type=F32)
            key_send[half, :, columns] = value.astype(BF16)

    key_sends = []
    key_own = []
    key_queue = []

    def key_out(half):
        place = wg_ref.at[0, :, w_columns(y, half)]
        for piece in range(PIECES):
            size = width // PIECES
            columns = pl.ds(piece * size, size)
            group = []
            for k in range(3):
                rows = pl.ds(pl.multiple_of(lax.rem(y + k + 1, 4) * keys, keys), keys)
                group.append(remote(key_send.at[half, rows, columns], place.at[:, columns], y_peers[k]))
            key_queue.append(group)
        key_own.append(local(key_send.at[half, my_keys], place))

    def pump(count=1, fresh=False):
        for _ in range(count):
            if not key_queue:
                return
            if not fresh:
                for copy in key_sends[-3 * DEPTH : len(key_sends) - 3 * (DEPTH - 1)]:
                    copy.wait_send()
                    sent.append(copy)
            key_sends.extend(start(key_queue.pop(0)))

    sent = []

    wait_recv(x_sends)
    wait_recv(g_far)
    key_half(0)
    key_out(0)
    key_half(1)
    key_out(1)
    own_half(0)
    pump(1, True)
    wait_recv(w_chunks[3])
    pump(DEPTH - 1, True)
    own_half(1)
    dot_sends = share(dots, jnp.concatenate([to_row(0), to_row(1)], axis=1))
    pump(3)
    wait(copies_c)
    wait_recv(dot_sends)
    slope = total_of(dots) * (inv_rms * inv_rms * inv_rms) / features

    def to_column(row):
        return jnp.transpose(jnp.broadcast_to(row, (128, row.shape[1])))

    shift_sends = []
    outs = [down_ref, up_ref]
    kept = [s > 0, s < n_sections - 1]
    for m in range(2):
        lanes[0] = to_column(inv_rms[:, m * tok : (m + 1) * tok])
        lanes[1] = to_column(slope[:, m * tok : (m + 1) * tok])

        @pl.loop(0, tok // row_block)
        def _(i):
            rows = pl.ds(pl.multiple_of(i * row_block, row_block), row_block)
            if m == 0:
                x_rows = x_all[h, rows].astype(F32)
            else:
                x_rows = x_far[rows].astype(F32)
            value = c_own[m, rows].astype(F32) + (
                hidden[m, rows] * lanes[0, rows, :1] - x_rows * lanes[1, rows, :1]
            )
            result[m, rows] = jnp.where(kept[m], value, 0.0).astype(BF16)

        shift_sends += start([remote(result.at[m], outs[m].at[0], (behind, ahead)[m])])
        pump(1)
    pump(len(key_queue))

    wait_recv(shift_sends)
    wait_recv(key_sends)
    wait(key_own)
    groups = [g_sends, x_sends, square_sends, part_sends, g_far, key_sends, dot_sends, shift_sends] + w_chunks
    for group in groups:
        for copy in group:
            if not any(copy is other for other in sent):
                copy.wait_send()


def per_device(*args, n_sections):
    w, _, xd, _, gd = args[:5]
    tok, width = xd.shape[1:]
    keys = gd.shape[2]
    hbm_spec = pl.BlockSpec(memory_space=pltpu.HBM)
    any_spec = pl.BlockSpec(memory_space=pl.ANY)
    vmem = pltpu.VMEM
    args = [pltpu.with_memory_space_constraint(a, pltpu.HBM) for a in args]
    outs = pl.pallas_call(
        functools.partial(kernel, n_sections),
        out_shape=(
            jax.ShapeDtypeStruct(w.shape, BF16),
            jax.ShapeDtypeStruct(xd.shape, BF16),
            jax.ShapeDtypeStruct(xd.shape, BF16),
        ),
        in_specs=[hbm_spec] * 8,
        out_specs=(any_spec,) * 3,
        scratch_shapes=[
            vmem((2, 2, 4 * keys, width), BF16),
            vmem((2, tok, 4 * keys), BF16),
            vmem((3, 4 * keys, tok), BF16),
            vmem((2, 2 * tok, width), BF16),
            vmem((tok, width), BF16),
            vmem((2, tok, width), BF16),
            vmem((2, tok, width), BF16),
            vmem((2, tok, width), BF16),
            vmem((2, tok, width), F32),
            vmem((2, 4 * keys, width), BF16),
            vmem((2, tok, width), BF16),
            vmem((2, tok, 128), F32),
            vmem((8, 8, 128), F32),
            vmem((8, 8, 128), F32),
            pltpu.SemaphoreType.DMA((N_SEMS,)),
            pltpu.SemaphoreType.DMA((N_SEMS,)),
            pltpu.SemaphoreType.DMA((32,)),
        ],
        compiler_params=pltpu.CompilerParams(
            collective_id=0, has_side_effects=True, vmem_limit_bytes=40 * 2**20
        ),
        name="relay_backward",
    )(*args)
    return outs


def solution(mesh):
    keys_split = P("section", "tp", None)
    features_split = P("section", None, "tp")
    return jax.shard_map(
        functools.partial(per_device, n_sections=mesh.shape["section"]),
        mesh=mesh,
        in_specs=(keys_split,) * 2 + (features_split,) * 6,
        out_specs=(keys_split, features_split, features_split),
        check_vma=False,
    )
```

```python
import functools

import jax
import jax.numpy as jnp
from jax import lax
from jax.experimental import pallas as pl
from jax.experimental.pallas import tpu as pltpu
from jax.sharding import PartitionSpec as P

epsilon = 1e-05
MESH = pl.DeviceIdType.MESH
K_PIECES = 8
X_PIECES = 4
DEPTH = 4
F32 = jnp.float32
BF16 = jnp.bfloat16
N_SEMS = 128


def kernel(
    n_sections,
    w_ref,
    mw_ref,
    xd_ref,
    cd_ref,
    gd_ref,
    xu_ref,
    cu_ref,
    gu_ref,
    wg_ref,
    down_ref,
    up_ref,
    w_all,
    g_all,
    g_scaled,
    x_all,
    x_far,
    x_relay,
    c_own,
    part_send,
    part_recv,
    hidden,
    key_send,
    result,
    lanes,
    squares,
    dots,
    ssem,
    rsem,
    lsem,
    ack,
):
    tok, width = x_far.shape
    keys = gd_ref.shape[2]
    features = width * 8
    tile = min(256, width)
    groups = tok // 128
    s = lax.axis_index("section")
    t = lax.axis_index("tp")
    y = t // 2
    h = t % 2
    pair = (s, t + 1 - 2 * h)
    y_peers = [(s, lax.rem(y + k, 4) * 2 + h) for k in range(1, 4)]
    t_peers = [(s, lax.rem(t + k, 8)) for k in range(1, 8)]
    mirror = n_sections - 1 - s
    mirrored = (mirror, t)
    z = s // 4
    turned = 8 * z + 3 - s
    relays = [(turned, t), (turned, t + 1 - 2 * h)]
    across_s = n_sections - 4 - 8 * z + s
    across = (across_s, t)
    behind = (lax.rem(s + n_sections - 1, n_sections), t)
    ahead = (lax.rem(s + 1, n_sections), t)

    others = [(s, k * 2 + 1 - h) for k in range(4)]

    barrier = pltpu.get_barrier_semaphore()
    low_half = h == 0
    low_mirror = s < n_sections // 2
    low_relay = s < turned

    def signal(semaphore, devices):
        for device in devices:
            pl.semaphore_signal(semaphore, inc=1, device_id=device, device_id_type=MESH)

    signal(barrier, y_peers)
    pl.when(low_half)(lambda: signal(barrier, others))
    pl.when(low_relay)(lambda: signal(barrier, relays))
    pl.when(low_mirror)(lambda: signal(barrier, [mirrored, across]))
    pl.when(s < n_sections - 1)(lambda: signal(barrier, [ahead]))

    used = [0]
    used_local = [0]

    def remote(src, dst, device):
        i = used[0]
        used[0] += 1
        return pltpu.make_async_remote_copy(
            src_ref=src,
            dst_ref=dst,
            send_sem=ssem.at[i],
            recv_sem=rsem.at[i],
            device_id=device,
            device_id_type=MESH,
        )

    def local(src, dst):
        i = used_local[0]
        used_local[0] += 1
        copy = pltpu.make_async_copy(src, dst, lsem.at[i])
        copy.start()
        return copy

    def start(copies):
        for copy in copies:
            copy.start()
        return copies

    def wait_recv(copies):
        for copy in copies:
            copy.wait_recv()

    def wait(copies):
        for copy in copies:
            copy.wait()

    y_queue = []
    y_started = []
    sent = []

    def pump(count=1):
        for _ in range(count):
            if len(y_started) >= DEPTH:
                for copy in y_started[-DEPTH]:
                    copy.wait_send()
                    sent.append(copy)
            y_started.append(start(y_queue.pop(0)))

    def cut(pieces, size):
        return [pl.ds(i * (size // pieces), size // pieces) for i in range(pieces)]

    def remote_cut(pieces, src, dst, device):
        return [remote(src.at[rows], dst.at[rows], device) for rows in cut(pieces, src.shape[0])]

    own_x = x_all.at[h, pl.ds(0, tok)]
    own_rows = [own_x, x_far]
    copies_x = [local(xd_ref.at[0], own_x), local(xu_ref.at[0], x_far)]
    my_keys = pl.ds(pl.multiple_of(y * keys, keys), keys)
    copies_g = [
        local(gd_ref.at[0], g_all.at[0, :, my_keys]),
        local(gu_ref.at[0], g_all.at[1, :, my_keys]),
    ]
    w_refs = [w_ref, mw_ref]
    halves = [1 - h, h]

    def w_columns(row, half):
        return pl.ds(pl.multiple_of((row * 2 + half) * width, width), width)

    copies_w = [
        [local(w_refs[m].at[0, :, w_columns(y, half)], w_all.at[m, i, my_keys]) for m in range(2)]
        for i, half in enumerate(halves)
    ]
    copies_c = [local(cd_ref.at[0], c_own.at[0]), local(cu_ref.at[0], c_own.at[1])]

    pl.semaphore_wait(barrier, 3 + jnp.where(low_half, 0, 4) + jnp.where(low_relay, 0, 2) + jnp.where(low_mirror, 0, 2) + jnp.where(s > 0, 1, 0))

    g_sends = start(
        [
            remote(ref.at[0], g_all.at[m, :, my_keys], device)
            for m, ref in enumerate((gd_ref, gu_ref))
            for device in y_peers
        ]
    )
    pl.when(h == 1)(lambda: signal(ack.at[0], others))
    pl.when(s > turned)(lambda: signal(ack.at[3], relays))
    pl.when(s >= n_sections // 2)(lambda: signal(ack.at[1], [mirrored, across]))
    pl.when(s > 0)(lambda: signal(ack.at[2], [behind]))

    def w_sends(m, i):
        return start(
            [
                remote(
                    w_refs[m].at[0, :, w_columns(lax.rem(y + k + 1, 4), halves[i])],
                    w_all.at[m, i, my_keys],
                    y_peers[k],
                )
                for k in range(3)
            ]
        )

    def to_row(m):
        return jnp.sum(jnp.transpose(lanes[m]), axis=0, keepdims=True)

    def fold(values):
        total = values[:, :128]
        for i in range(1, values.shape[1] // 128):
            total = total + values[:, i * 128 : (i + 1) * 128]
        return total

    def share(buffer, row):
        groups = row.shape[1] // 128
        buffer[t, :groups] = jnp.concatenate([row[:, i * 128 : (i + 1) * 128] for i in range(groups)], axis=0)
        return start([remote(buffer.at[t], buffer.at[t], device) for device in t_peers])

    def total_of(buffer, groups):
        total = buffer[0]
        for i in range(1, 8):
            total = total + buffer[i]
        return jnp.concatenate([total[i : i + 1] for i in range(groups)], axis=1)

    pl.when(low_half)(lambda: pl.semaphore_wait(ack.at[0], 4))
    pl.when(low_relay)(lambda: pl.semaphore_wait(ack.at[3], 2))
    row_halves = cut(2, tok)
    x_turned = []
    for i in range(2):
        x_turned.append(remote_cut(2, xu_ref.at[0, row_halves[i]], x_relay.at[row_halves[i]], relays[i]))
    for i in range(2):
        start([x_turned[1][i], x_turned[0][i]])

    row_block = min(64, tok)
    for m in range(2):
        copies_x[m].wait()

        @pl.loop(0, tok // row_block)
        def _(i):
            rows = pl.ds(pl.multiple_of(i * row_block, row_block), row_block)
            if m == 0:
                values = x_all[h, rows].astype(F32)
            else:
                values = x_far[rows].astype(F32)
            lanes[m, rows] = fold(values * values)

    square_sends = share(squares, jnp.concatenate([to_row(0), to_row(1)], axis=1))
    w_chunks = {(m, i): w_sends(m, i) for i in range(2) for m in range(2)}
    far_rows = [x_all.at[(h, 1 - h)[i], pl.ds(tok + rows.start, rows.size)] for i, rows in enumerate(row_halves)]
    x_mirror = [remote_cut(2, x_relay.at[row_halves[i]], far_rows[i], across) for i in range(2)]
    pl.when(low_mirror)(lambda: pl.semaphore_wait(ack.at[1], 2))
    for i in range(2):
        x_turned[1][i].wait_recv()
        x_mirror[1][i].start()

    wait_recv(x_turned[0])
    x_near = start(remote_cut(X_PIECES, xd_ref.at[0], own_x, pair))

    wait(copies_g)
    wait_recv(g_sends)

    def partial(m, i, use):
        copies_w[i][m].wait()
        wait_recv(w_chunks[m, i])

        @pl.loop(0, width // tile)
        def _(j):
            columns = pl.ds(pl.multiple_of(j * tile, tile), tile)
            use(columns, jnp.dot(g_all[m], w_all[m, i, :, columns], preferred_element_type=F32))

    def scale_g():
        wait_recv(square_sends)
        inv_rms = lax.rsqrt(total_of(squares, 2 * groups) / features + epsilon)
        for m in range(2):
            scale = inv_rms[:, m * tok : (m + 1) * tok]
            for k in range(4):
                block = jnp.transpose(g_all[m, :, k * keys : (k + 1) * keys].astype(F32))
                g_scaled[m, k * keys : (k + 1) * keys] = (block * scale).astype(BF16)
        return inv_rms

    inv_rms = scale_g()
    part_sends = []
    for m in range(2):

        def keep(columns, value):
            part_send[m, :, columns] = value.astype(BF16)

        if m == 1:
            wait_recv(x_mirror[1])
            x_pair = [start(remote_cut(2, far_rows[1], far_rows[1], pair))]
        partial(m, 0, keep)
        part_sends.append(start(remote_cut(X_PIECES, part_send.at[m], part_recv.at[m], pair)))
        if m == 0:
            start(x_mirror[0])
            g_far = start([remote(g_scaled.at[1], g_scaled.at[2], mirrored)])
    def own_half(m):
        def finish(columns, value):
            if m == 0:
                x_rows = x_all[h, :tok, columns]
            else:
                x_rows = x_far[:, columns]
            value = value + part_recv[m, :, columns].astype(F32)
            hidden[m, :, columns] = value
            lanes[m] += fold(value * x_rows.astype(F32))

        lanes[m] = jnp.zeros_like(lanes[m])
        wait_recv(part_sends[m])
        partial(m, 1, finish)

    def key_half(half):
        @pl.loop(0, width // tile)
        def _(j):
            columns = pl.ds(pl.multiple_of(j * tile, tile), tile)
            value = jnp.dot(g_scaled[0], x_all[half, :tok, columns], preferred_element_type=F32)
            value += jnp.dot(g_scaled[2], x_all[half, tok:, columns], preferred_element_type=F32)
            key_send[half, :, columns] = value.astype(BF16)

    key_sends = []
    key_own = []

    def key_out(half):
        place = wg_ref.at[0, :, w_columns(y, half)]
        for rows in cut(K_PIECES, keys):
            group = []
            for k in range(3):
                mine = pl.ds(pl.multiple_of(lax.rem(y + k + 1, 4) * keys + rows.start, rows.size), rows.size)
                group.append(remote(key_send.at[half, mine], place.at[rows], y_peers[k]))
            y_queue.append(group)
            key_sends.extend(group)
        key_own.append(local(key_send.at[half, my_keys], place))

    def to_column(row):
        return jnp.transpose(jnp.broadcast_to(row, (128, row.shape[1])))

    shift_sends = []
    outs = [down_ref, up_ref]
    kept = [s > 0, s < n_sections - 1]

    def finish_rows(m):
        wait_recv(dot_sends[m])
        copies_c[m].wait()
        scale = inv_rms[:, m * tok : (m + 1) * tok]
        lanes[0] = to_column(scale)
        lanes[1] = to_column(total_of(dots.at[m], groups) * (scale * scale * scale) / features)

        @pl.loop(0, tok // row_block)
        def _(i):
            rows = pl.ds(pl.multiple_of(i * row_block, row_block), row_block)
            if m == 0:
                x_rows = x_all[h, rows].astype(F32)
            else:
                x_rows = x_far[rows].astype(F32)
            value = c_own[m, rows].astype(F32) + (
                hidden[m, rows] * lanes[0, rows, :1] - x_rows * lanes[1, rows, :1]
            )
            result[m, rows] = jnp.where(kept[m], value, 0.0).astype(BF16)

        if m == 1:
            pl.when(s < n_sections - 1)(lambda: pl.semaphore_wait(ack.at[2], 1))
        shift_sends.extend(start([remote(result.at[m], outs[m].at[0], (behind, ahead)[m])]))

    own_half(0)
    dot_sends = [share(dots.at[0], to_row(0))]
    wait_recv(x_mirror[0])
    x_pair.append(start(remote_cut(2, far_rows[0], far_rows[0], pair)))
    wait_recv(g_far)
    wait_recv(x_pair[0])
    key_half(h)
    key_out(h)
    pump(DEPTH)
    own_half(1)
    dot_sends.append(share(dots.at[1], to_row(1)))
    pump(2)
    finish_rows(0)
    pump(2)
    wait_recv(x_near)
    wait_recv(x_pair[1])
    key_half(1 - h)
    key_out(1 - h)
    pump(2)
    finish_rows(1)
    pump(len(y_queue))
    wait_recv(shift_sends)
    wait_recv(key_sends)
    wait(key_own)
    groups = [g_sends, x_near, *x_turned, *x_mirror, *x_pair, square_sends, *part_sends, g_far, key_sends, *dot_sends, shift_sends, *w_chunks.values()]
    for group in groups:
        for copy in group:
            if not any(copy is other for other in sent):
                copy.wait_send()


def place(values):
    def body(*refs):
        sems = refs[-1]
        copies = [pltpu.make_async_copy(refs[i], refs[i + 3], sems.at[i]) for i in range(3)]
        for copy in copies:
            copy.start()
        for copy in copies:
            copy.wait()

    return pl.pallas_call(
        body,
        out_shape=tuple(jax.ShapeDtypeStruct(v.shape, v.dtype) for v in values),
        in_specs=[pl.BlockSpec(memory_space=pl.ANY)] * 3,
        out_specs=(pl.BlockSpec(memory_space=pltpu.HBM),) * 3,
        scratch_shapes=[pltpu.SemaphoreType.DMA((3,))],
        compiler_params=pltpu.CompilerParams(vmem_limit_bytes=2**20),
        name="place",
    )(*values)


def per_device(*args, n_sections):
    w, _, xd, _, gd = args[:5]
    tok, width = xd.shape[1:]
    keys = gd.shape[2]
    hbm_spec = pl.BlockSpec(memory_space=pltpu.HBM)
    any_spec = pl.BlockSpec(memory_space=pl.ANY)
    vmem = pltpu.VMEM
    args = [pltpu.with_memory_space_constraint(a, pltpu.HBM) for a in args]
    outs = pl.pallas_call(
        functools.partial(kernel, n_sections),
        out_shape=(
            jax.ShapeDtypeStruct(w.shape, BF16),
            jax.ShapeDtypeStruct(xd.shape, BF16),
            jax.ShapeDtypeStruct(xd.shape, BF16),
        ),
        in_specs=[hbm_spec] * 8,
        out_specs=(any_spec,) * 3,
        scratch_shapes=[
            vmem((2, 2, 4 * keys, width), BF16),
            vmem((2, tok, 4 * keys), BF16),
            vmem((3, 4 * keys, tok), BF16),
            vmem((2, 2 * tok, width), BF16),
            vmem((tok, width), BF16),
            vmem((tok, width), BF16),
            vmem((2, tok, width), BF16),
            vmem((2, tok, width), BF16),
            vmem((2, tok, width), BF16),
            vmem((2, tok, width), F32),
            vmem((2, 4 * keys, width), BF16),
            vmem((2, tok, width), BF16),
            vmem((2, tok, 128), F32),
            vmem((8, 8, 128), F32),
            vmem((2, 8, 8, 128), F32),
            pltpu.SemaphoreType.DMA((N_SEMS,)),
            pltpu.SemaphoreType.DMA((N_SEMS,)),
            pltpu.SemaphoreType.DMA((16,)),
            pltpu.SemaphoreType.REGULAR((4,)),
        ],
        compiler_params=pltpu.CompilerParams(
            collective_id=0, has_side_effects=True, vmem_limit_bytes=40 * 2**20
        ),
        name="relay_backward",
    )(*args)
    return place(outs)


def solution(mesh):
    keys_split = P("section", "tp", None)
    features_split = P("section", None, "tp")
    return jax.shard_map(
        functools.partial(per_device, n_sections=mesh.shape["section"]),
        mesh=mesh,
        in_specs=(keys_split,) * 2 + (features_split,) * 6,
        out_specs=(keys_split, features_split, features_split),
        check_vma=False,
    )
```

```python
import functools

import jax
import jax.numpy as jnp
from jax import lax
from jax.experimental import pallas as pl
from jax.experimental.pallas import tpu as pltpu
from jax.sharding import PartitionSpec as P

epsilon = 1e-05
MESH = pl.DeviceIdType.MESH
F32 = jnp.float32
BF16 = jnp.bfloat16
N_SEMS = 128


def kernel(
    n_sections,
    w_ref,
    mw_ref,
    xd_ref,
    cd_ref,
    gd_ref,
    xu_ref,
    cu_ref,
    gu_ref,
    wg_ref,
    down_ref,
    up_ref,
    w_all,
    g_all,
    g_scaled,
    x_all,
    x_far,
    x_relay,
    zeros,
    c_own,
    part_send,
    part_recv,
    hidden,
    key_send,
    result,
    lanes,
    squares,
    dots,
    ssem,
    rsem,
    lsem,
    ack,
):
    tok, width = x_far.shape
    keys = gd_ref.shape[2]
    features = width * 8
    tile = min(256, width)
    groups = tok // 128
    s = lax.axis_index("section")
    t = lax.axis_index("tp")
    y = t // 2
    h = t % 2
    pair = (s, t + 1 - 2 * h)
    y_peers = [(s, lax.rem(y + k, 4) * 2 + h) for k in range(1, 4)]
    t_peers = [(s, lax.rem(t + k, 8)) for k in range(1, 8)]
    mirror = n_sections - 1 - s
    mirrored = (mirror, t)
    z = s // 4
    turned = 8 * z + 3 - s
    relays = [(turned, t), (turned, t + 1 - 2 * h)]
    across_s = n_sections - 4 - 8 * z + s
    across = (across_s, t)
    behind = (lax.rem(s + n_sections - 1, n_sections), t)
    ahead = (lax.rem(s + 1, n_sections), t)

    others = [(s, k * 2 + 1 - h) for k in range(4)]

    barrier = pltpu.get_barrier_semaphore()
    low_half = h == 0
    low_mirror = s < n_sections // 2
    low_relay = s < turned

    def signal(semaphore, devices):
        for device in devices:
            pl.semaphore_signal(semaphore, inc=1, device_id=device, device_id_type=MESH)

    signal(barrier, y_peers)
    pl.when(low_half)(lambda: signal(barrier, others))
    pl.when(low_relay)(lambda: signal(barrier, relays))
    pl.when(low_mirror)(lambda: signal(barrier, [mirrored, across]))
    pl.when(s < n_sections - 1)(lambda: signal(barrier, [ahead]))

    used = [0]
    used_local = [0]

    def remote(src, dst, device):
        i = used[0]
        used[0] += 1
        return pltpu.make_async_remote_copy(
            src_ref=src,
            dst_ref=dst,
            send_sem=ssem.at[i],
            recv_sem=rsem.at[i],
            device_id=device,
            device_id_type=MESH,
        )

    def local(src, dst):
        i = used_local[0]
        used_local[0] += 1
        copy = pltpu.make_async_copy(src, dst, lsem.at[i])
        copy.start()
        return copy

    def start(copies):
        for copy in copies:
            copy.start()
        return copies

    def wait_recv(copies):
        for copy in copies:
            copy.wait_recv()

    def wait(copies):
        for copy in copies:
            copy.wait()

    def cut(pieces, size):
        return [pl.ds(i * (size // pieces), size // pieces) for i in range(pieces)]

    def remote_cut(pieces, src, dst, device):
        return [remote(src.at[rows], dst.at[rows], device) for rows in cut(pieces, src.shape[0])]

    own_x = x_all.at[h, pl.ds(0, tok)]
    own_rows = [own_x, x_far]
    copies_x = [local(xd_ref.at[0], own_x), local(xu_ref.at[0], x_far)]
    my_keys = pl.ds(pl.multiple_of(y * keys, keys), keys)
    copies_g = [
        local(gd_ref.at[0], g_all.at[0, :, my_keys]),
        local(gu_ref.at[0], g_all.at[1, :, my_keys]),
    ]
    w_refs = [w_ref, mw_ref]
    halves = [1 - h, h]

    def w_columns(row, half):
        return pl.ds(pl.multiple_of((row * 2 + half) * width, width), width)

    copies_w = [
        [local(w_refs[m].at[0, :, w_columns(y, half)], w_all.at[m, i, my_keys]) for m in range(2)]
        for i, half in enumerate(halves)
    ]
    copies_c = [local(cd_ref.at[0], c_own.at[0]), local(cu_ref.at[0], c_own.at[1])]

    pl.semaphore_wait(barrier, 3 + jnp.where(low_half, 0, 4) + jnp.where(low_relay, 0, 2) + jnp.where(low_mirror, 0, 2) + jnp.where(s > 0, 1, 0))

    g_sends = start(
        [
            remote(ref.at[0], g_all.at[m, :, my_keys], device)
            for m, ref in enumerate((gd_ref, gu_ref))
            for device in (y_peers[0], y_peers[2])
        ]
    )
    pl.when(h == 1)(lambda: signal(ack.at[0], others))
    pl.when(s > turned)(lambda: signal(ack.at[3], relays))
    pl.when(s >= n_sections // 2)(lambda: signal(ack.at[1], [mirrored, across]))
    pl.when(s > 0)(lambda: signal(ack.at[2], [behind]))

    def w_sends(m, i):
        return start(
            [
                remote(
                    w_refs[m].at[0, :, w_columns(lax.rem(y + k + 1, 4), halves[i])],
                    w_all.at[m, i, my_keys],
                    y_peers[k],
                )
                for k in range(3)
            ]
        )

    def to_row(m):
        return jnp.sum(jnp.transpose(lanes[m]), axis=0, keepdims=True)

    def fold(values):
        total = values[:, :128]
        for i in range(1, values.shape[1] // 128):
            total = total + values[:, i * 128 : (i + 1) * 128]
        return total

    def share(buffer, row):
        groups = row.shape[1] // 128
        buffer[t, :groups] = jnp.concatenate([row[:, i * 128 : (i + 1) * 128] for i in range(groups)], axis=0)
        return start([remote(buffer.at[t], buffer.at[t], device) for device in t_peers])

    def total_of(buffer, groups):
        total = buffer[0]
        for i in range(1, 8):
            total = total + buffer[i]
        return jnp.concatenate([total[i : i + 1] for i in range(groups)], axis=1)

    copies_zero = [pltpu.make_async_copy(zeros, ref.at[0], lsem.at[14 + m]) for m, ref in enumerate((down_ref, up_ref))]
    for m, at_end in enumerate((s == n_sections - 1, s == 0)):

        @pl.when(at_end)
        def _():
            zeros[...] = jnp.zeros_like(zeros)
            copies_zero[m].start()

    pl.when(low_half)(lambda: pl.semaphore_wait(ack.at[0], 4))
    pl.when(low_relay)(lambda: pl.semaphore_wait(ack.at[3], 2))
    row_halves = cut(2, tok)
    x_turned = []
    for i in range(2):
        x_turned.append(remote_cut(2, xu_ref.at[0, row_halves[i]], x_relay.at[row_halves[i]], relays[i]))
    for i in range(2):
        start([x_turned[1][i], x_turned[0][i]])

    row_block = min(64, tok)
    for m in range(2):
        copies_x[m].wait()

        @pl.loop(0, tok // row_block)
        def _(i):
            rows = pl.ds(pl.multiple_of(i * row_block, row_block), row_block)
            if m == 0:
                values = x_all[h, rows].astype(F32)
            else:
                values = x_far[rows].astype(F32)
            lanes[m, rows] = fold(values * values)

    square_sends = share(squares, jnp.concatenate([to_row(0), to_row(1)], axis=1))
    w_chunks = {(0, 0): w_sends(0, 0)}
    far_rows = [x_all.at[(h, 1 - h)[i], pl.ds(tok + rows.start, rows.size)] for i, rows in enumerate(row_halves)]
    x_mirror = [remote_cut(2, x_relay.at[row_halves[i]], far_rows[i], across) for i in range(2)]
    pl.when(low_mirror)(lambda: pl.semaphore_wait(ack.at[1], 2))
    wait(copies_g)
    wait_recv(g_sends)
    g_passed = []
    for m in range(2):
        for i, step in enumerate((1, 3)):
            columns = pl.ds(pl.multiple_of(lax.rem(y + step, 4) * keys, keys), keys)
            block = g_all.at[m, row_halves[i], columns]
            g_passed.append(remote(block, block, y_peers[2 - 2 * i]))
    start(g_passed)
    for m, i in ((1, 0), (0, 1), (1, 1)):
        w_chunks[m, i] = w_sends(m, i)
    for i in range(2):
        x_turned[1][i].wait_recv()
        x_mirror[1][i].start()

    wait_recv(x_turned[0])
    x_near = start([remote(xd_ref.at[0], own_x, pair)])

    wait_recv(g_passed)

    def partial(m, i, use):
        copies_w[i][m].wait()
        wait_recv(w_chunks[m, i])

        @pl.loop(0, width // tile)
        def _(j):
            columns = pl.ds(pl.multiple_of(j * tile, tile), tile)
            use(columns, jnp.dot(g_all[m], w_all[m, i, :, columns], preferred_element_type=F32))

    def scale_g():
        wait_recv(square_sends)
        inv_rms = lax.rsqrt(total_of(squares, 2 * groups) / features + epsilon)
        for m in range(2):
            scale = inv_rms[:, m * tok : (m + 1) * tok]
            for k in range(4):
                block = jnp.transpose(g_all[m, :, k * keys : (k + 1) * keys].astype(F32))
                g_scaled[m, k * keys : (k + 1) * keys] = (block * scale).astype(BF16)
        return inv_rms

    inv_rms = scale_g()
    part_sends = []
    for m in range(2):

        def keep(columns, value):
            part_send[m, :, columns] = value.astype(BF16)

        if m == 1:
            wait_recv(x_mirror[1])
            x_pair = start([remote(far_rows[1], far_rows[1], pair)])
        partial(m, 0, keep)
        part_sends.append(start([remote(part_send.at[m], part_recv.at[m], pair)]))
        if m == 0:
            start(x_mirror[0])
            g_far = start([remote(g_scaled.at[1], g_scaled.at[2], mirrored)])
    def own_half(m):
        def finish(columns, value):
            if m == 0:
                x_rows = x_all[h, :tok, columns]
            else:
                x_rows = x_far[:, columns]
            value = value + part_recv[m, :, columns].astype(F32)
            hidden[m, :, columns] = value
            lanes[m] += fold(value * x_rows.astype(F32))

        lanes[m] = jnp.zeros_like(lanes[m])
        wait_recv(part_sends[m])
        partial(m, 1, finish)

    key_sends = []
    key_own = []

    def key_quarter(half, part):
        size = width // 2

        @pl.loop(0, size // tile)
        def _(j):
            columns = pl.ds(pl.multiple_of(part * size + j * tile, tile), tile)
            value = jnp.dot(g_scaled[0], x_all[half, :tok, columns], preferred_element_type=F32)
            value += jnp.dot(g_scaled[2], x_all[half, tok:, columns], preferred_element_type=F32)
            key_send[half, :, columns] = value.astype(BF16)

        columns = pl.ds(part * size, size)
        place = wg_ref.at[0, :, pl.ds(pl.multiple_of((y * 2 + half) * width + part * size, size), size)]
        for k in range(3):
            rows = pl.ds(pl.multiple_of(lax.rem(y + k + 1, 4) * keys, keys), keys)
            key_sends.extend(start([remote(key_send.at[half, rows, columns], place, y_peers[k])]))
        key_own.append(local(key_send.at[half, my_keys, columns], place))

    def to_column(row):
        return jnp.transpose(jnp.broadcast_to(row, (128, row.shape[1])))

    shift_sends = []
    outs = [down_ref, up_ref]
    kept = [s > 0, s < n_sections - 1]

    def finish_rows(m):
        wait_recv(dot_sends[m])
        copies_c[m].wait()
        scale = inv_rms[:, m * tok : (m + 1) * tok]
        lanes[0] = to_column(scale)
        lanes[1] = to_column(total_of(dots.at[m], groups) * (scale * scale * scale) / features)

        @pl.loop(0, tok // row_block)
        def _(i):
            rows = pl.ds(pl.multiple_of(i * row_block, row_block), row_block)
            if m == 0:
                x_rows = x_all[h, rows].astype(F32)
            else:
                x_rows = x_far[rows].astype(F32)
            value = c_own[m, rows].astype(F32) + (
                hidden[m, rows] * lanes[0, rows, :1] - x_rows * lanes[1, rows, :1]
            )
            result[m, rows] = value.astype(BF16)

        if m == 1:
            pl.when(s < n_sections - 1)(lambda: pl.semaphore_wait(ack.at[2], 1))
        copy = remote(result.at[m], outs[m].at[0], (behind, ahead)[m])
        pl.when(kept[m])(copy.start)
        shift_sends.append(copy)

    own_half(0)
    dot_sends = [share(dots.at[0], to_row(0))]
    wait_recv(x_mirror[0])
    for part in range(2):
        block = far_rows[0].at[:, pl.ds(part * (width // 2), width // 2)]
        x_pair += start([remote(block, block, pair)])
    wait_recv(g_far)
    x_pair[0].wait_recv()
    key_quarter(h, 0)
    key_quarter(h, 1)
    own_half(1)
    dot_sends.append(share(dots.at[1], to_row(1)))
    finish_rows(0)
    wait_recv(x_near)
    for part in range(2):
        x_pair[1 + part].wait_recv()
        key_quarter(1 - h, part)
    finish_rows(1)

    for group in [g_sends, g_passed, x_near, *x_turned, *x_mirror, x_pair, square_sends, *part_sends, g_far, *dot_sends]:
        for copy in group:
            copy.wait_send()
    for group in w_chunks.values():
        for copy in group:
            copy.wait_send()
    for m in range(2):
        pl.when(kept[1 - m])(shift_sends[m].wait_recv)
        pl.when(kept[m])(shift_sends[m].wait_send)

        @pl.when(jnp.logical_not(kept[1 - m]))
        def _():
            copies_zero[m].wait()

    wait_recv(key_sends)
    wait(key_own)
    for copy in key_sends:
        copy.wait_send()


def place(values):
    def body(*refs):
        sems = refs[-1]
        copies = [pltpu.make_async_copy(refs[i], refs[i + 3], sems.at[i]) for i in range(3)]
        for copy in copies:
            copy.start()
        for copy in copies:
            copy.wait()

    return pl.pallas_call(
        body,
        out_shape=tuple(jax.ShapeDtypeStruct(v.shape, v.dtype) for v in values),
        in_specs=[pl.BlockSpec(memory_space=pl.ANY)] * 3,
        out_specs=(pl.BlockSpec(memory_space=pltpu.HBM),) * 3,
        scratch_shapes=[pltpu.SemaphoreType.DMA((3,))],
        compiler_params=pltpu.CompilerParams(vmem_limit_bytes=2**20),
        name="place",
    )(*values)


def per_device(*args, n_sections):
    w, _, xd, _, gd = args[:5]
    tok, width = xd.shape[1:]
    keys = gd.shape[2]
    hbm_spec = pl.BlockSpec(memory_space=pltpu.HBM)
    any_spec = pl.BlockSpec(memory_space=pl.ANY)
    vmem = pltpu.VMEM
    args = [pltpu.with_memory_space_constraint(a, pltpu.HBM) for a in args]
    outs = pl.pallas_call(
        functools.partial(kernel, n_sections),
        out_shape=(
            jax.ShapeDtypeStruct(w.shape, BF16),
            jax.ShapeDtypeStruct(xd.shape, BF16),
            jax.ShapeDtypeStruct(xd.shape, BF16),
        ),
        in_specs=[hbm_spec] * 8,
        out_specs=(any_spec,) * 3,
        scratch_shapes=[
            vmem((2, 2, 4 * keys, width), BF16),
            vmem((2, tok, 4 * keys), BF16),
            vmem((3, 4 * keys, tok), BF16),
            vmem((2, 2 * tok, width), BF16),
            vmem((tok, width), BF16),
            vmem((tok, width), BF16),
            vmem((tok, width), BF16),
            vmem((2, tok, width), BF16),
            vmem((2, tok, width), BF16),
            vmem((2, tok, width), BF16),
            vmem((2, tok, width), F32),
            vmem((2, 4 * keys, width), BF16),
            vmem((2, tok, width), BF16),
            vmem((2, tok, 128), F32),
            vmem((8, 8, 128), F32),
            vmem((2, 8, 8, 128), F32),
            pltpu.SemaphoreType.DMA((N_SEMS,)),
            pltpu.SemaphoreType.DMA((N_SEMS,)),
            pltpu.SemaphoreType.DMA((16,)),
            pltpu.SemaphoreType.REGULAR((4,)),
        ],
        compiler_params=pltpu.CompilerParams(
            collective_id=0, has_side_effects=True, vmem_limit_bytes=40 * 2**20
        ),
        name="relay_backward",
    )(*args)
    return place(outs)


def solution(mesh):
    keys_split = P("section", "tp", None)
    features_split = P("section", None, "tp")
    return jax.shard_map(
        functools.partial(per_device, n_sections=mesh.shape["section"]),
        mesh=mesh,
        in_specs=(keys_split,) * 2 + (features_split,) * 6,
        out_specs=(keys_split, features_split, features_split),
        check_vma=False,
    )
```

```python
import functools

import jax
import jax.numpy as jnp
from jax import lax
from jax.experimental import pallas as pl
from jax.experimental.pallas import tpu as pltpu
from jax.sharding import PartitionSpec as P

epsilon = 1e-05
MESH = pl.DeviceIdType.MESH
F32 = jnp.float32
BF16 = jnp.bfloat16
N_SEMS = 70


def kernel(
    n_sections,
    w_ref,
    mw_ref,
    xd_ref,
    cd_ref,
    gd_ref,
    xu_ref,
    cu_ref,
    gu_ref,
    wg_ref,
    down_ref,
    up_ref,
    w_all,
    g_all,
    g_scaled,
    x_all,
    x_far,
    x_relay,
    zeros,
    c_own,
    part_send,
    part_recv,
    hidden,
    key_send,
    result,
    lanes,
    squares,
    dots,
    ssem,
    rsem,
    lsem,
    ack,
):
    tok, width = x_far.shape
    keys = gd_ref.shape[2]
    features = width * 8
    tile = min(256, width)
    groups = tok // 128
    s = lax.axis_index("section")
    t = lax.axis_index("tp")
    y = t // 2
    h = t % 2
    pair = (s, t + 1 - 2 * h)
    y_peers = [(s, lax.rem(y + k, 4) * 2 + h) for k in range(1, 4)]
    t_peers = [(s, lax.rem(t + k, 8)) for k in range(1, 8)]
    mirror = n_sections - 1 - s
    mirrored = (mirror, t)
    z = s // 4
    z_quarter = lax.rem(z, n_sections // 8)
    at_turn = jnp.logical_or(z_quarter == 0, z_quarter == n_sections // 8 - 1)
    turned = 8 * z + 3 - s
    relays = [(turned, t), (turned, t + 1 - 2 * h)]
    across_s = n_sections - 4 - 8 * z + s
    across = (across_s, t)
    behind = (lax.rem(s + n_sections - 1, n_sections), t)
    ahead = (lax.rem(s + 1, n_sections), t)

    others = [(s, k * 2 + 1 - h) for k in range(4)]

    barrier = pltpu.get_barrier_semaphore()
    low_half = h == 0
    low_mirror = s < n_sections // 2
    low_relay = s < turned

    def signal(semaphore, devices):
        for device in devices:
            pl.semaphore_signal(semaphore, inc=1, device_id=device, device_id_type=MESH)

    signal(barrier, y_peers)
    pl.when(low_half)(lambda: signal(barrier, others))
    pl.when(low_relay)(lambda: signal(barrier, relays))
    pl.when(low_mirror)(lambda: signal(barrier, [mirrored, across]))
    pl.when(s < n_sections - 1)(lambda: signal(barrier, [ahead]))

    used = [0]
    used_local = [0]

    def remote(src, dst, device):
        i = used[0]
        used[0] += 1
        return pltpu.make_async_remote_copy(
            src_ref=src,
            dst_ref=dst,
            send_sem=ssem.at[i],
            recv_sem=rsem.at[i],
            device_id=device,
            device_id_type=MESH,
        )

    def local(src, dst):
        i = used_local[0]
        used_local[0] += 1
        copy = pltpu.make_async_copy(src, dst, lsem.at[i])
        copy.start()
        return copy

    def start(copies):
        for copy in copies:
            copy.start()
        return copies

    def wait_recv(copies):
        for copy in copies:
            copy.wait_recv()

    def wait(copies):
        for copy in copies:
            copy.wait()

    def cut(pieces, size):
        return [pl.ds(i * (size // pieces), size // pieces) for i in range(pieces)]

    def remote_cut(pieces, src, dst, device):
        return [remote(src.at[rows], dst.at[rows], device) for rows in cut(pieces, src.shape[0])]

    own_x = x_all.at[h, pl.ds(0, tok)]
    own_rows = [own_x, x_far]
    copies_x = [local(xd_ref.at[0], own_x), local(xu_ref.at[0], x_far)]
    my_keys = pl.ds(pl.multiple_of(y * keys, keys), keys)
    copies_g = [
        local(gd_ref.at[0], g_all.at[0, :, my_keys]),
        local(gu_ref.at[0], g_all.at[1, :, my_keys]),
    ]
    w_refs = [w_ref, mw_ref]
    halves = [1 - h, h]

    def w_columns(row, half):
        return pl.ds(pl.multiple_of((row * 2 + half) * width, width), width)

    copies_w = [
        [local(w_refs[m].at[0, :, w_columns(y, half)], w_all.at[m, i, my_keys]) for m in range(2)]
        for i, half in enumerate(halves)
    ]
    copies_c = [local(cd_ref.at[0], c_own.at[0]), local(cu_ref.at[0], c_own.at[1])]

    pl.semaphore_wait(barrier, 3 + jnp.where(low_half, 0, 4) + jnp.where(low_relay, 0, 2) + jnp.where(low_mirror, 0, 2) + jnp.where(s > 0, 1, 0))

    g_sends = start(
        [
            remote(ref.at[0], g_all.at[m, :, my_keys], device)
            for m, ref in enumerate((gd_ref, gu_ref))
            for device in (y_peers[0], y_peers[2])
        ]
    )
    pl.when(h == 1)(lambda: signal(ack.at[0], others))
    pl.when(s > turned)(lambda: signal(ack.at[3], relays))
    pl.when(s >= n_sections // 2)(lambda: signal(ack.at[1], [mirrored, across]))
    pl.when(s > 0)(lambda: signal(ack.at[2], [behind]))

    def w_sends(m, i):
        return start(
            [
                remote(
                    w_refs[m].at[0, :, w_columns(lax.rem(y + k + 1, 4), halves[i])],
                    w_all.at[m, i, my_keys],
                    y_peers[k],
                )
                for k in range(3)
            ]
        )

    def to_row(m):
        return jnp.sum(jnp.transpose(lanes[m]), axis=0, keepdims=True)

    def fold(values):
        total = values[:, :128]
        for i in range(1, values.shape[1] // 128):
            total = total + values[:, i * 128 : (i + 1) * 128]
        return total

    def share(buffer, row):
        groups = row.shape[1] // 128
        buffer[t, :groups] = jnp.concatenate([row[:, i * 128 : (i + 1) * 128] for i in range(groups)], axis=0)
        return start([remote(buffer.at[t], buffer.at[t], device) for device in t_peers])

    def total_of(buffer, groups):
        total = buffer[0]
        for i in range(1, 8):
            total = total + buffer[i]
        return jnp.concatenate([total[i : i + 1] for i in range(groups)], axis=1)

    copies_zero = [pltpu.make_async_copy(zeros, ref.at[0], lsem.at[14 + m]) for m, ref in enumerate((down_ref, up_ref))]
    for m, at_end in enumerate((s == n_sections - 1, s == 0)):

        @pl.when(at_end)
        def _():
            zeros[...] = jnp.zeros_like(zeros)
            copies_zero[m].start()

    pl.when(low_half)(lambda: pl.semaphore_wait(ack.at[0], 4))
    pl.when(low_relay)(lambda: pl.semaphore_wait(ack.at[3], 2))
    row_halves = cut(2, tok)
    x_turned = []
    for i in range(2):
        x_turned.append(remote_cut(2, xu_ref.at[0, row_halves[i]], x_relay.at[row_halves[i]], relays[i]))
    for i in range(2):
        start([x_turned[1][i], x_turned[0][i]])

    row_block = min(64, tok)
    for m in range(2):
        copies_x[m].wait()

        @pl.loop(0, tok // row_block)
        def _(i):
            rows = pl.ds(pl.multiple_of(i * row_block, row_block), row_block)
            if m == 0:
                values = x_all[h, rows].astype(F32)
            else:
                values = x_far[rows].astype(F32)
            lanes[m, rows] = fold(values * values)

    square_sends = share(squares, jnp.concatenate([to_row(0), to_row(1)], axis=1))
    w_chunks = {(0, 0): w_sends(0, 0)}
    far_rows = [x_all.at[(h, 1 - h)[i], pl.ds(tok + rows.start, rows.size)] for i, rows in enumerate(row_halves)]
    x_mirror = [remote_cut(2, x_relay.at[row_halves[i]], far_rows[i], across) for i in range(2)]
    pl.when(low_mirror)(lambda: pl.semaphore_wait(ack.at[1], 2))
    wait(copies_g)
    wait_recv(g_sends)
    g_passed = []
    for m in range(2):
        for i, step in enumerate((1, 3)):
            columns = pl.ds(pl.multiple_of(lax.rem(y + step, 4) * keys, keys), keys)
            block = g_all.at[m, row_halves[i], columns]
            g_passed.append(remote(block, block, y_peers[2 - 2 * i]))
    start(g_passed)
    for m, i in ((1, 0), (0, 1), (1, 1)):
        w_chunks[m, i] = w_sends(m, i)
    for i in range(2):
        x_turned[1][i].wait_recv()
        x_mirror[1][i].start()
        if i == 0:
            x_turned[0][0].wait_recv()
            x_near = start([remote(xd_ref.at[0], own_x, pair)])
    x_turned[0][1].wait_recv()

    wait_recv(g_passed)

    def partial(m, i, use):
        copies_w[i][m].wait()
        wait_recv(w_chunks[m, i])

        @pl.loop(0, width // tile)
        def _(j):
            columns = pl.ds(pl.multiple_of(j * tile, tile), tile)
            use(columns, jnp.dot(g_all[m], w_all[m, i, :, columns], preferred_element_type=F32))

    def scale_g():
        wait_recv(square_sends)
        inv_rms = lax.rsqrt(total_of(squares, 2 * groups) / features + epsilon)
        for m in range(2):
            scale = inv_rms[:, m * tok : (m + 1) * tok]
            for k in range(4):
                block = jnp.transpose(g_all[m, :, k * keys : (k + 1) * keys].astype(F32))
                g_scaled[m, k * keys : (k + 1) * keys] = (block * scale).astype(BF16)
        return inv_rms

    inv_rms = scale_g()
    part_sends = []
    for m in range(2):

        def keep(columns, value):
            part_send[m, :, columns] = value.astype(BF16)

        if m == 1:
            wait_recv(x_mirror[1])
            x_pair = start([remote(far_rows[1], far_rows[1], pair)])
        partial(m, 0, keep)
        part_sends.append(start([remote(part_send.at[m], part_recv.at[m], pair)]))
        if m == 0:
            pl.when(at_turn)(lambda: [None, start(x_mirror[0])][0])
            g_far = start([remote(g_scaled.at[1], g_scaled.at[2], mirrored)])
    pl.when(jnp.logical_not(at_turn))(lambda: [None, start(x_mirror[0])][0])

    def own_half(m):
        def finish(columns, value):
            if m == 0:
                x_rows = x_all[h, :tok, columns]
            else:
                x_rows = x_far[:, columns]
            value = value + part_recv[m, :, columns].astype(F32)
            hidden[m, :, columns] = value
            lanes[m] += fold(value * x_rows.astype(F32))

        lanes[m] = jnp.zeros_like(lanes[m])
        wait_recv(part_sends[m])
        partial(m, 1, finish)

    key_sends = []
    key_own = []

    def key_quarter(half, part):
        size = width // 2

        @pl.loop(0, size // tile)
        def _(j):
            columns = pl.ds(pl.multiple_of(part * size + j * tile, tile), tile)
            value = jnp.dot(g_scaled[0], x_all[half, :tok, columns], preferred_element_type=F32)
            value += jnp.dot(g_scaled[2], x_all[half, tok:, columns], preferred_element_type=F32)
            key_send[half, :, columns] = value.astype(BF16)

        columns = pl.ds(part * size, size)
        place = wg_ref.at[0, :, pl.ds(pl.multiple_of((y * 2 + half) * width + part * size, size), size)]
        for k in range(3):
            rows = pl.ds(pl.multiple_of(lax.rem(y + k + 1, 4) * keys, keys), keys)
            key_sends.extend(start([remote(key_send.at[half, rows, columns], place, y_peers[k])]))
        key_own.append(local(key_send.at[half, my_keys, columns], place))

    def to_column(row):
        return jnp.transpose(jnp.broadcast_to(row, (128, row.shape[1])))

    shift_sends = []
    outs = [down_ref, up_ref]
    kept = [s > 0, s < n_sections - 1]

    def finish_rows(m):
        wait_recv(dot_sends[m])
        copies_c[m].wait()
        scale = inv_rms[:, m * tok : (m + 1) * tok]
        lanes[0] = to_column(scale)
        lanes[1] = to_column(total_of(dots.at[m], groups) * (scale * scale * scale) / features)

        @pl.loop(0, tok // row_block)
        def _(i):
            rows = pl.ds(pl.multiple_of(i * row_block, row_block), row_block)
            if m == 0:
                x_rows = x_all[h, rows].astype(F32)
            else:
                x_rows = x_far[rows].astype(F32)
            value = c_own[m, rows].astype(F32) + (
                hidden[m, rows] * lanes[0, rows, :1] - x_rows * lanes[1, rows, :1]
            )
            result[m, rows] = value.astype(BF16)

        if m == 1:
            pl.when(s < n_sections - 1)(lambda: pl.semaphore_wait(ack.at[2], 1))
        copy = remote(result.at[m], outs[m].at[0], (behind, ahead)[m])
        pl.when(kept[m])(copy.start)
        shift_sends.append(copy)

    own_half(0)
    dot_sends = [share(dots.at[0], to_row(0))]
    wait_recv(x_mirror[0])
    for part in range(2):
        block = far_rows[0].at[:, pl.ds(part * (width // 2), width // 2)]
        x_pair += start([remote(block, block, pair)])
    wait_recv(g_far)
    x_pair[0].wait_recv()
    key_quarter(h, 0)
    key_quarter(h, 1)
    own_half(1)
    dot_sends.append(share(dots.at[1], to_row(1)))
    finish_rows(0)
    wait_recv(x_near)
    for part in range(2):
        x_pair[1 + part].wait_recv()
        key_quarter(1 - h, part)
    finish_rows(1)

    for group in [g_sends, g_passed, x_near, *x_turned, *x_mirror, x_pair, square_sends, *part_sends, g_far, *dot_sends]:
        for copy in group:
            copy.wait_send()
    for group in w_chunks.values():
        for copy in group:
            copy.wait_send()
    for m in range(2):
        pl.when(kept[1 - m])(shift_sends[m].wait_recv)
        pl.when(kept[m])(shift_sends[m].wait_send)

        @pl.when(jnp.logical_not(kept[1 - m]))
        def _():
            copies_zero[m].wait()

    wait_recv(key_sends)
    wait(key_own)
    for copy in key_sends:
        copy.wait_send()


def place(values):
    def body(*refs):
        sems = refs[-1]
        copies = [pltpu.make_async_copy(refs[i], refs[i + 3], sems.at[i]) for i in range(3)]
        for copy in copies:
            copy.start()
        for copy in copies:
            copy.wait()

    return pl.pallas_call(
        body,
        out_shape=tuple(jax.ShapeDtypeStruct(v.shape, v.dtype) for v in values),
        in_specs=[pl.BlockSpec(memory_space=pl.ANY)] * 3,
        out_specs=(pl.BlockSpec(memory_space=pltpu.HBM),) * 3,
        scratch_shapes=[pltpu.SemaphoreType.DMA((3,))],
        compiler_params=pltpu.CompilerParams(vmem_limit_bytes=2**20),
        name="place",
    )(*values)


def per_device(*args, n_sections):
    w, _, xd, _, gd = args[:5]
    tok, width = xd.shape[1:]
    keys = gd.shape[2]
    hbm_spec = pl.BlockSpec(memory_space=pltpu.HBM)
    any_spec = pl.BlockSpec(memory_space=pl.ANY)
    vmem = pltpu.VMEM
    args = [pltpu.with_memory_space_constraint(a, pltpu.HBM) for a in args]
    outs = pl.pallas_call(
        functools.partial(kernel, n_sections),
        out_shape=(
            jax.ShapeDtypeStruct(w.shape, BF16),
            jax.ShapeDtypeStruct(xd.shape, BF16),
            jax.ShapeDtypeStruct(xd.shape, BF16),
        ),
        in_specs=[hbm_spec] * 8,
        out_specs=(any_spec,) * 3,
        scratch_shapes=[
            vmem((2, 2, 4 * keys, width), BF16),
            vmem((2, tok, 4 * keys), BF16),
            vmem((3, 4 * keys, tok), BF16),
            vmem((2, 2 * tok, width), BF16),
            vmem((tok, width), BF16),
            vmem((tok, width), BF16),
            vmem((tok, width), BF16),
            vmem((2, tok, width), BF16),
            vmem((2, tok, width), BF16),
            vmem((2, tok, width), BF16),
            vmem((2, tok, width), F32),
            vmem((2, 4 * keys, width), BF16),
            vmem((2, tok, width), BF16),
            vmem((2, tok, 128), F32),
            vmem((8, 8, 128), F32),
            vmem((2, 8, 8, 128), F32),
            pltpu.SemaphoreType.DMA((N_SEMS,)),
            pltpu.SemaphoreType.DMA((N_SEMS,)),
            pltpu.SemaphoreType.DMA((16,)),
            pltpu.SemaphoreType.REGULAR((4,)),
        ],
        compiler_params=pltpu.CompilerParams(
            collective_id=0, has_side_effects=True, vmem_limit_bytes=40 * 2**20
        ),
        name="relay_backward",
    )(*args)
    return place(outs)


def solution(mesh):
    keys_split = P("section", "tp", None)
    features_split = P("section", None, "tp")
    return jax.shard_map(
        functools.partial(per_device, n_sections=mesh.shape["section"]),
        mesh=mesh,
        in_specs=(keys_split,) * 2 + (features_split,) * 6,
        out_specs=(keys_split, features_split, features_split),
        check_vma=False,
    )
```

```python
import functools

import jax
import jax.numpy as jnp
from jax import lax
from jax.experimental import pallas as pl
from jax.experimental.pallas import tpu as pltpu
from jax.sharding import PartitionSpec as P

epsilon = 1e-05
MESH = pl.DeviceIdType.MESH
F32 = jnp.float32
BF16 = jnp.bfloat16
N_SEMS = 70


def kernel(
    n_sections,
    w_ref,
    mw_ref,
    xd_ref,
    cd_ref,
    gd_ref,
    xu_ref,
    cu_ref,
    gu_ref,
    wg_ref,
    down_ref,
    up_ref,
    w_all,
    g_all,
    g_scaled,
    x_all,
    x_far,
    x_relay,
    zeros,
    c_own,
    part_send,
    part_recv,
    hidden,
    key_send,
    result,
    lanes,
    squares,
    dots,
    ssem,
    rsem,
    lsem,
    ack,
):
    tok, width = x_far.shape
    keys = gd_ref.shape[2]
    features = width * 8
    tile = min(256, width)
    groups = tok // 128
    s = lax.axis_index("section")
    t = lax.axis_index("tp")
    y = t // 2
    h = t % 2
    pair = (s, t + 1 - 2 * h)
    y_peers = [(s, lax.rem(y + k, 4) * 2 + h) for k in range(1, 4)]
    t_peers = [(s, lax.rem(t + k, 8)) for k in range(1, 8)]
    mirror = n_sections - 1 - s
    mirrored = (mirror, t)
    z = s // 4
    z_quarter = lax.rem(z, n_sections // 8)
    at_turn = jnp.logical_or(z_quarter == 0, z_quarter == n_sections // 8 - 1)
    turned = 8 * z + 3 - s
    relays = [(turned, t), (turned, t + 1 - 2 * h)]
    across_s = n_sections - 4 - 8 * z + s
    across = (across_s, t)
    behind = (lax.rem(s + n_sections - 1, n_sections), t)
    ahead = (lax.rem(s + 1, n_sections), t)

    others = [(s, k * 2 + 1 - h) for k in range(4)]

    barrier = pltpu.get_barrier_semaphore()
    low_half = h == 0
    low_mirror = s < n_sections // 2
    low_relay = s < turned

    def signal(semaphore, devices):
        for device in devices:
            pl.semaphore_signal(semaphore, inc=1, device_id=device, device_id_type=MESH)

    signal(barrier, y_peers)
    pl.when(low_half)(lambda: signal(barrier, others))
    pl.when(low_relay)(lambda: signal(barrier, relays))
    pl.when(low_mirror)(lambda: signal(barrier, [mirrored, across]))
    pl.when(s < n_sections - 1)(lambda: signal(barrier, [ahead]))

    used = [0]
    used_local = [0]

    def remote(src, dst, device):
        i = used[0]
        used[0] += 1
        return pltpu.make_async_remote_copy(
            src_ref=src,
            dst_ref=dst,
            send_sem=ssem.at[i],
            recv_sem=rsem.at[i],
            device_id=device,
            device_id_type=MESH,
        )

    def local(src, dst):
        i = used_local[0]
        used_local[0] += 1
        copy = pltpu.make_async_copy(src, dst, lsem.at[i])
        copy.start()
        return copy

    def start(copies):
        for copy in copies:
            copy.start()
        return copies

    def wait_recv(copies):
        for copy in copies:
            copy.wait_recv()

    def wait(copies):
        for copy in copies:
            copy.wait()

    def cut(pieces, size):
        return [pl.ds(i * (size // pieces), size // pieces) for i in range(pieces)]

    def remote_cut(pieces, src, dst, device):
        return [remote(src.at[rows], dst.at[rows], device) for rows in cut(pieces, src.shape[0])]

    own_x = x_all.at[h, pl.ds(0, tok)]
    own_rows = [own_x, x_far]
    copies_x = [local(xd_ref.at[0], own_x), local(xu_ref.at[0], x_far)]
    my_keys = pl.ds(pl.multiple_of(y * keys, keys), keys)
    copies_g = [
        local(gd_ref.at[0], g_all.at[0, :, my_keys]),
        local(gu_ref.at[0], g_all.at[1, :, my_keys]),
    ]
    w_refs = [w_ref, mw_ref]
    halves = [1 - h, h]

    def w_columns(row, half):
        return pl.ds(pl.multiple_of((row * 2 + half) * width, width), width)

    copies_w = [
        [local(w_refs[m].at[0, :, w_columns(y, half)], w_all.at[m, i, my_keys]) for m in range(2)]
        for i, half in enumerate(halves)
    ]
    copies_c = [local(cd_ref.at[0], c_own.at[0]), local(cu_ref.at[0], c_own.at[1])]

    pl.semaphore_wait(barrier, 3 + jnp.where(low_half, 0, 4) + jnp.where(low_relay, 0, 2) + jnp.where(low_mirror, 0, 2) + jnp.where(s > 0, 1, 0))

    g_sends = start(
        [
            remote(ref.at[0], g_all.at[m, :, my_keys], device)
            for m, ref in enumerate((gd_ref, gu_ref))
            for device in (y_peers[0], y_peers[2])
        ]
    )
    pl.when(h == 1)(lambda: signal(ack.at[0], others))
    pl.when(s > turned)(lambda: signal(ack.at[3], relays))
    pl.when(s >= n_sections // 2)(lambda: signal(ack.at[1], [mirrored, across]))
    pl.when(s > 0)(lambda: signal(ack.at[2], [behind]))

    def w_sends(m, i):
        return start(
            [
                remote(
                    w_refs[m].at[0, :, w_columns(lax.rem(y + k + 1, 4), halves[i])],
                    w_all.at[m, i, my_keys],
                    y_peers[k],
                )
                for k in range(3)
            ]
        )

    def to_row(m):
        return jnp.sum(jnp.transpose(lanes[m]), axis=0, keepdims=True)

    def fold(values):
        total = values[:, :128]
        for i in range(1, values.shape[1] // 128):
            total = total + values[:, i * 128 : (i + 1) * 128]
        return total

    def share(buffer, row):
        groups = row.shape[1] // 128
        buffer[t, :groups] = jnp.concatenate([row[:, i * 128 : (i + 1) * 128] for i in range(groups)], axis=0)
        return start([remote(buffer.at[t], buffer.at[t], device) for device in t_peers])

    def total_of(buffer, groups):
        total = buffer[0]
        for i in range(1, 8):
            total = total + buffer[i]
        return jnp.concatenate([total[i : i + 1] for i in range(groups)], axis=1)

    copies_zero = [pltpu.make_async_copy(zeros, ref.at[0], lsem.at[14 + m]) for m, ref in enumerate((down_ref, up_ref))]
    for m, at_end in enumerate((s == n_sections - 1, s == 0)):

        @pl.when(at_end)
        def _():
            zeros[...] = jnp.zeros_like(zeros)
            copies_zero[m].start()

    pl.when(low_half)(lambda: pl.semaphore_wait(ack.at[0], 4))
    pl.when(low_relay)(lambda: pl.semaphore_wait(ack.at[3], 2))
    row_halves = cut(2, tok)
    x_turned = []
    for i in range(2):
        x_turned.append(remote_cut(2, xu_ref.at[0, row_halves[i]], x_relay.at[row_halves[i]], relays[i]))
    for i in range(2):
        start([x_turned[1][i], x_turned[0][i]])

    row_block = min(64, tok)
    for m in range(2):
        copies_x[m].wait()

        @pl.loop(0, tok // row_block)
        def _(i):
            rows = pl.ds(pl.multiple_of(i * row_block, row_block), row_block)
            if m == 0:
                values = x_all[h, rows].astype(F32)
            else:
                values = x_far[rows].astype(F32)
            lanes[m, rows] = fold(values * values)

    square_sends = share(squares, jnp.concatenate([to_row(0), to_row(1)], axis=1))
    w_chunks = {(0, 0): w_sends(0, 0)}
    far_rows = [x_all.at[(h, 1 - h)[i], pl.ds(tok + rows.start, rows.size)] for i, rows in enumerate(row_halves)]
    x_mirror = [remote_cut(2, x_relay.at[row_halves[i]], far_rows[i], across) for i in range(2)]
    pl.when(low_mirror)(lambda: pl.semaphore_wait(ack.at[1], 2))
    wait(copies_g)
    wait_recv(g_sends)
    g_passed = []
    for m in range(2):
        for i, step in enumerate((1, 3)):
            columns = pl.ds(pl.multiple_of(lax.rem(y + step, 4) * keys, keys), keys)
            block = g_all.at[m, row_halves[i], columns]
            g_passed.append(remote(block, block, y_peers[2 - 2 * i]))
    start(g_passed)
    for m, i in ((1, 0), (0, 1), (1, 1)):
        w_chunks[m, i] = w_sends(m, i)
    for i in range(2):
        x_turned[1][i].wait_recv()
        x_mirror[1][i].start()
        if i == 0:
            x_turned[0][0].wait_recv()
            x_near = start([remote(xd_ref.at[0], own_x, pair)])
    x_turned[0][1].wait_recv()

    wait_recv(g_passed)

    def partial(m, i, use):
        copies_w[i][m].wait()
        wait_recv(w_chunks[m, i])

        @pl.loop(0, width // tile)
        def _(j):
            columns = pl.ds(pl.multiple_of(j * tile, tile), tile)
            use(columns, jnp.dot(g_all[m], w_all[m, i, :, columns], preferred_element_type=F32))

    def scale_g():
        wait_recv(square_sends)
        inv_rms = lax.rsqrt(total_of(squares, 2 * groups) / features + epsilon)
        for m in range(2):
            scale = inv_rms[:, m * tok : (m + 1) * tok]
            for k in range(4):
                block = jnp.transpose(g_all[m, :, k * keys : (k + 1) * keys].astype(F32))
                g_scaled[m, k * keys : (k + 1) * keys] = (block * scale).astype(BF16)
        return inv_rms

    inv_rms = scale_g()
    g_far = start([remote(g_scaled.at[1], g_scaled.at[2], mirrored)])
    part_sends = []
    for m in range(2):

        def keep(columns, value):
            part_send[m, :, columns] = value.astype(BF16)

        if m == 1:
            wait_recv(x_mirror[1])
            x_pair = start([remote(far_rows[1], far_rows[1], pair)])
        partial(m, 0, keep)
        part_sends.append(start([remote(part_send.at[m], part_recv.at[m], pair)]))
        if m == 0:
            pl.when(at_turn)(lambda: [None, start(x_mirror[0])][0])
    pl.when(jnp.logical_not(at_turn))(lambda: [None, start(x_mirror[0])][0])

    def own_half(m):
        def finish(columns, value):
            if m == 0:
                x_rows = x_all[h, :tok, columns]
            else:
                x_rows = x_far[:, columns]
            value = value + part_recv[m, :, columns].astype(F32)
            hidden[m, :, columns] = value
            lanes[m] += fold(value * x_rows.astype(F32))

        lanes[m] = jnp.zeros_like(lanes[m])
        wait_recv(part_sends[m])
        partial(m, 1, finish)

    key_sends = []
    key_own = []

    def key_quarter(half, part):
        size = width // 2

        @pl.loop(0, size // tile)
        def _(j):
            columns = pl.ds(pl.multiple_of(part * size + j * tile, tile), tile)
            value = jnp.dot(g_scaled[0], x_all[half, :tok, columns], preferred_element_type=F32)
            value += jnp.dot(g_scaled[2], x_all[half, tok:, columns], preferred_element_type=F32)
            key_send[half, :, columns] = value.astype(BF16)

        columns = pl.ds(part * size, size)
        place = wg_ref.at[0, :, pl.ds(pl.multiple_of((y * 2 + half) * width + part * size, size), size)]
        for k in range(3):
            rows = pl.ds(pl.multiple_of(lax.rem(y + k + 1, 4) * keys, keys), keys)
            key_sends.extend(start([remote(key_send.at[half, rows, columns], place, y_peers[k])]))
        key_own.append(local(key_send.at[half, my_keys, columns], place))

    def to_column(row):
        return jnp.transpose(jnp.broadcast_to(row, (128, row.shape[1])))

    shift_sends = []
    outs = [down_ref, up_ref]
    kept = [s > 0, s < n_sections - 1]

    def finish_rows(m):
        wait_recv(dot_sends[m])
        copies_c[m].wait()
        scale = inv_rms[:, m * tok : (m + 1) * tok]
        lanes[0] = to_column(scale)
        lanes[1] = to_column(total_of(dots.at[m], groups) * (scale * scale * scale) / features)

        @pl.loop(0, tok // row_block)
        def _(i):
            rows = pl.ds(pl.multiple_of(i * row_block, row_block), row_block)
            if m == 0:
                x_rows = x_all[h, rows].astype(F32)
            else:
                x_rows = x_far[rows].astype(F32)
            value = c_own[m, rows].astype(F32) + (
                hidden[m, rows] * lanes[0, rows, :1] - x_rows * lanes[1, rows, :1]
            )
            result[m, rows] = value.astype(BF16)

        if m == 1:
            pl.when(s < n_sections - 1)(lambda: pl.semaphore_wait(ack.at[2], 1))
        copy = remote(result.at[m], outs[m].at[0], (behind, ahead)[m])
        pl.when(kept[m])(copy.start)
        shift_sends.append(copy)

    own_half(0)
    dot_sends = [share(dots.at[0], to_row(0))]
    wait_recv(x_mirror[0])
    wait_recv(g_far)
    x_pair[0].wait_recv()
    key_quarter(h, 0)
    key_quarter(h, 1)
    for part in range(2):
        block = far_rows[0].at[:, pl.ds(part * (width // 2), width // 2)]
        x_pair += start([remote(block, block, pair)])
    own_half(1)
    dot_sends.append(share(dots.at[1], to_row(1)))
    finish_rows(0)
    wait_recv(x_near)
    for part in range(2):
        x_pair[1 + part].wait_recv()
        key_quarter(1 - h, part)
    finish_rows(1)

    for group in [g_sends, g_passed, x_near, *x_turned, *x_mirror, x_pair, square_sends, *part_sends, g_far, *dot_sends]:
        for copy in group:
            copy.wait_send()
    for group in w_chunks.values():
        for copy in group:
            copy.wait_send()
    for m in range(2):
        pl.when(kept[1 - m])(shift_sends[m].wait_recv)
        pl.when(kept[m])(shift_sends[m].wait_send)

        @pl.when(jnp.logical_not(kept[1 - m]))
        def _():
            copies_zero[m].wait()

    wait_recv(key_sends)
    wait(key_own)
    for copy in key_sends:
        copy.wait_send()


def place(values):
    def body(*refs):
        sems = refs[-1]
        copies = [pltpu.make_async_copy(refs[i], refs[i + 3], sems.at[i]) for i in range(3)]
        for copy in copies:
            copy.start()
        for copy in copies:
            copy.wait()

    return pl.pallas_call(
        body,
        out_shape=tuple(jax.ShapeDtypeStruct(v.shape, v.dtype) for v in values),
        in_specs=[pl.BlockSpec(memory_space=pl.ANY)] * 3,
        out_specs=(pl.BlockSpec(memory_space=pltpu.HBM),) * 3,
        scratch_shapes=[pltpu.SemaphoreType.DMA((3,))],
        compiler_params=pltpu.CompilerParams(vmem_limit_bytes=2**20),
        name="place",
    )(*values)


def per_device(*args, n_sections):
    w, _, xd, _, gd = args[:5]
    tok, width = xd.shape[1:]
    keys = gd.shape[2]
    hbm_spec = pl.BlockSpec(memory_space=pltpu.HBM)
    any_spec = pl.BlockSpec(memory_space=pl.ANY)
    vmem = pltpu.VMEM
    args = [pltpu.with_memory_space_constraint(a, pltpu.HBM) for a in args]
    outs = pl.pallas_call(
        functools.partial(kernel, n_sections),
        out_shape=(
            jax.ShapeDtypeStruct(w.shape, BF16),
            jax.ShapeDtypeStruct(xd.shape, BF16),
            jax.ShapeDtypeStruct(xd.shape, BF16),
        ),
        in_specs=[hbm_spec] * 8,
        out_specs=(any_spec,) * 3,
        scratch_shapes=[
            vmem((2, 2, 4 * keys, width), BF16),
            vmem((2, tok, 4 * keys), BF16),
            vmem((3, 4 * keys, tok), BF16),
            vmem((2, 2 * tok, width), BF16),
            vmem((tok, width), BF16),
            vmem((tok, width), BF16),
            vmem((tok, width), BF16),
            vmem((2, tok, width), BF16),
            vmem((2, tok, width), BF16),
            vmem((2, tok, width), BF16),
            vmem((2, tok, width), F32),
            vmem((2, 4 * keys, width), BF16),
            vmem((2, tok, width), BF16),
            vmem((2, tok, 128), F32),
            vmem((8, 8, 128), F32),
            vmem((2, 8, 8, 128), F32),
            pltpu.SemaphoreType.DMA((N_SEMS,)),
            pltpu.SemaphoreType.DMA((N_SEMS,)),
            pltpu.SemaphoreType.DMA((16,)),
            pltpu.SemaphoreType.REGULAR((4,)),
        ],
        compiler_params=pltpu.CompilerParams(
            collective_id=0, has_side_effects=True, vmem_limit_bytes=40 * 2**20
        ),
        name="relay_backward",
    )(*args)
    return place(outs)


def solution(mesh):
    keys_split = P("section", "tp", None)
    features_split = P("section", None, "tp")
    return jax.shard_map(
        functools.partial(per_device, n_sections=mesh.shape["section"]),
        mesh=mesh,
        in_specs=(keys_split,) * 2 + (features_split,) * 6,
        out_specs=(keys_split, features_split, features_split),
        check_vma=False,
    )
```
